256 devices in a mesh: blk: 16 (over y_hi, z), group: 16 (over x, y_lo, core).
Axes of the slice: x: 4, y: 4 (y_hi: 2, y_lo: 2; y = y_hi * 2 + y_lo), z: 8, core: 2. Of those that a mesh axis runs over, the one named last changes fastest.
Arguments:
- images: bfloat16 [163840, 1152], P(('blk', 'group')), may hold values from -0.1796875 to 0.1796875
- texts: bfloat16 [163840, 1152], P(('blk', 'group')), may hold values from -0.1796875 to 0.1796875
- image_ids: int32 [163840], P(('blk', 'group')), may hold values from 0 to 255
- text_ids: int32 [163840], P(('blk', 'group')), may hold values from 0 to 255
- logit_scale: float32 [1], replicated, may hold values from 5 to 12
- logit_bias: float32 [1], replicated, may hold values from -4 to -1
Outputs:
- row_loss: float32 [163840], P(('blk', 'group'))
- image_grad: float32 [163840, 1152], P(('blk', 'group'))
- text_grad: float32 [163840, 1152], P(('blk', 'group'))
The draws below stay inside these ranges and needn't reach their ends.
All inputs are finite; a program needn't handle non-finite values.
Results may differ from the reference program's by a relative error of at most 0.0052.
Values may be sent and summed in bfloat16 or wider, within the bound.
No kernel may reach another device: no remote copies, remote signals or barrier semaphores. Data moves between devices by JAX's collectives and lax.ppermute only.
A program may use at most 64 MiB of HBM per device.

```python
import jax
import jax.numpy as jnp
from jax import lax

D = 1152
ROWS = 640
PAIRS = 256
NROWS = 163840
N_BLK = 16
N_GROUP = 16


def with_ends(array, key, least, high):
    spot = [jax.random.randint(jax.random.fold_in(key, axis), (), 0, length) for axis, length in enumerate(array.shape)]
    main_axis = array.shape.index(max(array.shape))
    neighbour = spot[:main_axis] + [(spot[main_axis] + 1) % array.shape[main_axis]] + spot[main_axis + 1:]
    return array.at[tuple(spot)].set(least).at[tuple(neighbour)].set(high)


def block_levels(rng, shape, split, least, high):
    loudness = 1.0
    for dim, blocks in split:
        heights = jax.random.uniform(jax.random.fold_in(jax.random.fold_in(rng, 6), dim), (blocks,), jnp.float32, least / len(split), high / len(split))
        loudness = loudness * jnp.repeat(jnp.exp(heights), shape[dim] // blocks).reshape((-1,) + (1,) * (len(shape) - 1 - dim))
    return loudness


def noise(key, extent, spread, limit, shards=(), kind=jnp.bfloat16):
    factor_of = block_levels(key, extent, shards, -0.22, 0.18) if shards else 1.0
    entries = jax.random.normal(key, extent, jnp.float32) * spread * factor_of
    return jnp.minimum(jnp.maximum(entries, -limit), limit).astype(kind)


def setup_inputs(seed: int = 0) -> dict:
    splits = jax.random.split(jax.random.key(seed), 7)
    images = noise(splits[0], (NROWS, D), 0.03, 0.1796875, ((0, 256),))
    texts = noise(splits[1], (NROWS, D), 0.03, 0.1796875, ((0, 256),))
    image_ids = with_ends(jax.random.randint(splits[2], (NROWS,), 0, PAIRS), jax.random.fold_in(splits[2], 1), 0, PAIRS - 1).astype(jnp.int32)
    text_ids = with_ends(jax.random.randint(splits[3], (NROWS,), 0, PAIRS), jax.random.fold_in(splits[3], 1), 0, PAIRS - 1).astype(jnp.int32)
    logit_scale = jnp.clip(jax.random.uniform(splits[4], (1,), jnp.float32, 5.0, 12.0), 5.0, 12.0)
    logit_bias = jnp.clip(jax.random.uniform(splits[5], (1,), jnp.float32, -4.0, -1.0), -4.0, -1.0)
    return {"images": images, "texts": texts, "image_ids": image_ids, "text_ids": text_ids, "logit_scale": logit_scale, "logit_bias": logit_bias}


def unit_rows(values):
    full = values.astype(jnp.float32)
    norms = jnp.sqrt(lax.optimization_barrier(jnp.sum(full * full, axis=-1, keepdims=True)) + 1e-06)
    return (full / norms, norms)

def reference(images, texts, image_ids, text_ids, logit_scale, logit_bias):
    width = images.shape[1]
    image_unit, image_norm = unit_rows(images)
    text_unit, text_norm = unit_rows(texts)
    image_bf = image_unit.astype(jnp.bfloat16).reshape(N_BLK, N_GROUP, ROWS, width)
    text_bf = text_unit.astype(jnp.bfloat16).reshape(N_BLK, N_GROUP, ROWS, width)
    img_ids = image_ids.reshape(N_BLK, N_GROUP, ROWS)
    txt_ids = text_ids.reshape(N_BLK, N_GROUP, ROWS)
    scale = logit_scale[0]
    bias = logit_bias[0]

    def one_block(index):
        pos_b = index // N_GROUP
        pos_g = index % N_GROUP
        xb = image_bf[pos_b, pos_g]
        xid = img_ids[pos_b, pos_g]
        sources = [(pos_b, pos_g), ((pos_b - 1) % N_BLK, pos_g), ((pos_b - 2) % N_BLK, pos_g), (pos_b, (pos_g - 1) % N_GROUP)]
        grad_sum = jnp.zeros((ROWS, width), jnp.float32)
        loss_sum = jnp.zeros((ROWS,), jnp.float32)
        partials = []
        for src_b, src_g in sources:
            yb = text_bf[src_b, src_g]
            yid = txt_ids[src_b, src_g]
            logits = scale * jnp.dot(xb, yb.T, preferred_element_type=jnp.float32) + bias
            signs = jnp.where(xid[:, None] == yid[None, :], 1.0, -1.0).astype(jnp.float32)
            loss_sum = loss_sum + lax.optimization_barrier(jnp.sum(jax.nn.softplus(-signs * logits), axis=1))
            coef = (-signs * scale * jax.nn.sigmoid(-signs * logits)).astype(jnp.bfloat16)
            grad_sum = grad_sum + jnp.dot(coef, yb, preferred_element_type=jnp.float32)
            partials.append(jnp.dot(coef.T, xb, preferred_element_type=jnp.float32).astype(jnp.bfloat16))
        return (loss_sum / (4 * ROWS), grad_sum, jnp.stack(partials))
    losses, unit_grads, partials = lax.map(one_block, jnp.arange(N_BLK * N_GROUP, dtype=jnp.int32))
    partials = partials.reshape(N_BLK, N_GROUP, 4, ROWS, width)

    def owner_sum(index):
        pos_b = index // N_GROUP
        pos_g = index % N_GROUP
        total = partials[pos_b, pos_g, 0].astype(jnp.float32)
        total = total + partials[(pos_b + 1) % N_BLK, pos_g, 1].astype(jnp.float32)
        total = total + partials[(pos_b + 2) % N_BLK, pos_g, 2].astype(jnp.float32)
        total = total + partials[pos_b, (pos_g + 1) % N_GROUP, 3].astype(jnp.float32)
        return total
    text_unit_grad = lax.map(owner_sum, jnp.arange(N_BLK * N_GROUP, dtype=jnp.int32)).reshape(-1, width)
    image_unit_grad = unit_grads.reshape(-1, width)
    image_grad = (image_unit_grad - image_unit * lax.optimization_barrier(jnp.sum(image_unit * image_unit_grad, axis=1, keepdims=True))) / image_norm
    text_grad = (text_unit_grad - text_unit * lax.optimization_barrier(jnp.sum(text_unit * text_unit_grad, axis=1, keepdims=True))) / text_norm
    return (losses.reshape(-1), image_grad, text_grad)
```

```python
import jax
import jax.numpy as jnp
from jax import lax
from jax.sharding import PartitionSpec as P


def passed_along(shard, axis, by):
    devices = lax.axis_size(axis)
    return lax.ppermute(shard, axis, [(i, (i + by) % devices) for i in range(devices)])


def unit_rows(values):
    full = values.astype(jnp.float32)
    norms = jnp.sqrt(jnp.sum(full * full, axis=-1, keepdims=True) + 1e-06)
    return (full / norms, norms)


def pair_terms(image_bf, image_ids, text_bf, text_ids, scale, bias):
    logits = scale * jnp.dot(image_bf, text_bf.T, preferred_element_type=jnp.float32) + bias
    signs = jnp.where(image_ids[:, None] == text_ids[None, :], 1.0, -1.0).astype(jnp.float32)
    score = -signs * logits
    coef = (-signs * scale * jax.nn.sigmoid(score)).astype(jnp.bfloat16)
    return score, coef


def image_side(coef, text_bf):
    return jnp.dot(coef, text_bf, preferred_element_type=jnp.float32)


def text_side(coef, image_bf):
    return lax.dot_general(coef, image_bf, (((0,), (0,)), ((), ())), preferred_element_type=jnp.float32)


def shards(images, texts, image_ids, text_ids, logit_scale, logit_bias):
    rows = images.shape[0]
    image_unit, image_norm = unit_rows(images)
    text_unit, text_norm = unit_rows(texts)
    image_bf = image_unit.astype(jnp.bfloat16)
    text_bf = text_unit.astype(jnp.bfloat16)
    scale = logit_scale[0]
    bias = logit_bias[0]
    near_text = passed_along(text_bf, "blk", 1)
    near_image = passed_along(image_bf, "blk", -1)
    hop_text = passed_along(text_bf, "group", 1)
    hop_image = passed_along(image_bf, "group", -1)
    near_tid = passed_along(text_ids, "blk", 1)
    near_iid = passed_along(image_ids, "blk", -1)
    hop_tid = passed_along(text_ids, "group", 1)
    hop_iid = passed_along(image_ids, "group", -1)
    far_tid = passed_along(text_ids, "blk", 2)
    far_iid = passed_along(image_ids, "blk", -2)
    far_text = passed_along(near_text, "blk", 1)
    far_image = passed_along(near_image, "blk", -1)

    score, coef = pair_terms(image_bf, image_ids, text_bf, text_ids, scale, bias)
    loss = jnp.sum(jax.nn.softplus(score), axis=1)
    image_unit_grad = image_side(coef, text_bf)
    text_unit_grad = text_side(coef, image_bf)
    for there, their_ids in ((near_text, near_tid), (hop_text, hop_tid), (far_text, far_tid)):
        score, coef = pair_terms(image_bf, image_ids, there, their_ids, scale, bias)
        loss = loss + jnp.sum(jax.nn.softplus(score), axis=1)
        image_unit_grad = image_unit_grad + image_side(coef, there)
    for there, their_ids in ((near_image, near_iid), (hop_image, hop_iid), (far_image, far_iid)):
        _, coef = pair_terms(there, their_ids, text_bf, text_ids, scale, bias)
        text_unit_grad = text_unit_grad + text_side(coef, there)
    row_loss = loss / (4 * rows)
    image_grad = (
        image_unit_grad - image_unit * jnp.sum(image_unit * image_unit_grad, axis=1, keepdims=True)
    ) / image_norm
    text_grad = (
        text_unit_grad - text_unit * jnp.sum(text_unit * text_unit_grad, axis=1, keepdims=True)
    ) / text_norm
    return (row_loss, image_grad, text_grad)


def solution(mesh):
    placed = (
        P(("blk", "group"), None),
        P(("blk", "group"), None),
        P(("blk", "group")),
        P(("blk", "group")),
        P(),
        P(),
    )
    return jax.shard_map(
        shards,
        mesh=mesh,
        in_specs=placed,
        out_specs=(P(("blk", "group")), P(("blk", "group"), None), P(("blk", "group"), None)),
        check_vma=False,
    )
```

```python
import functools

import jax
import jax.numpy as jnp
from jax import lax
from jax.experimental import pallas as pl
from jax.experimental.pallas import tpu as pltpu
from jax.sharding import PartitionSpec as P

WHOLE = pl.BlockSpec(memory_space=pltpu.VMEM)
SCALAR = pl.BlockSpec(memory_space=pltpu.SMEM)
ANYWHERE = pl.BlockSpec(memory_space=pl.ANY)
LANES = 128
ID_ROWS = 16
BAND = 320
PART = 160
F32, BF16 = jnp.float32, jnp.bfloat16
BOTH = ("blk", "group")


def routes(blks, groups):
    out = [[], [], [], []]
    for p in range(blks):
        for q in range(groups):
            here, up = p * groups + q, 1 if p % 2 == 0 else -1
            out[0].append((here, (p + up) % blks * groups + q))
            out[1].append((here, (p - up) % blks * groups + q))
            out[2].append((here, p * groups + (q + up) % groups))
            out[3].append((here, p * groups + (q - up) % groups))
    return out


def unit_rows(values):
    full = values.astype(F32)
    return full * lax.rsqrt(jnp.sum(full * full, axis=-1, keepdims=True) + 1e-06)


def projected(values, grad):
    full = values.astype(F32)
    scales = lax.rsqrt(jnp.sum(full * full, axis=-1, keepdims=True) + 1e-06)
    along = jnp.sum(full * grad, axis=1, keepdims=True)
    return grad * scales - full * (along * (scales * scales * scales))


def score_block(mine, theirs, my_ids, their_ids, scale, bias):
    dots = lax.dot_general(mine, theirs, (((1,), (1,)), ((), ())), preferred_element_type=F32)
    turn = jnp.where(my_ids == their_ids, -1.0, 1.0)
    power = jnp.exp(turn * (scale * dots + bias))
    whole = 1.0 + power
    coef = ((turn * scale) * (power * pl.reciprocal(whole, approx=True))).astype(BF16)
    return coef, power, whole


def softplus_sums(power, whole):
    values = jnp.where(power < 1e-3, power - 0.5 * power * power, jnp.log(whole))
    total = values[:, :LANES]
    for at in range(LANES, values.shape[1], LANES):
        total = total + values[:, at : at + LANES]
    return total


def bands(rows, size):
    return [slice(at, at + size) for at in range(0, rows, size)]


def id_row(packed, first, rows):
    at = packed.shape[0] - ID_ROWS
    return packed[at:, first : first + rows].astype(F32)[:1]


def even_blk():
    return lax.rem(lax.axis_index("blk"), 2) == 0


def prep_kernel(is_a, texts, images, text_ids, image_ids, packed, raw, sems):
    rows = raw.shape[0]
    texts_here = even_blk() if is_a else jnp.logical_not(even_blk())
    pieces = bands(rows, PART)

    @pl.when(texts_here)
    def _():
        for n, piece in enumerate(pieces):
            pltpu.make_async_copy(texts.at[piece], raw.at[piece], sems.at[n]).start()

    @pl.when(jnp.logical_not(texts_here))
    def _():
        for n, piece in enumerate(pieces):
            pltpu.make_async_copy(images.at[piece], raw.at[piece], sems.at[n]).start()

    ids = jnp.where(texts_here, text_ids[...].reshape(1, rows), image_ids[...].reshape(1, rows))
    packed[rows:] = jnp.zeros((ID_ROWS, packed.shape[1]), BF16)
    packed[rows:, :rows] = jnp.broadcast_to(ids.astype(F32), (ID_ROWS, rows)).astype(BF16)
    for n, piece in enumerate(pieces):
        pltpu.make_async_copy(texts.at[piece], raw.at[piece], sems.at[n]).wait()
        packed[piece] = unit_rows(raw[piece]).astype(BF16)


def add_band(mine, theirs, col, their_ids, sb, band):
    coef, power, whole = score_block(mine[band], theirs, col[band, :1], their_ids, sb[0], sb[1])
    return jnp.dot(coef, theirs, preferred_element_type=F32), softplus_sums(power, whole)


def own_kernel(a, b, sb, a_grad, b_grad, a_loss, b_loss, a_col, b_col):
    rows = a_grad.shape[0]
    a_row, b_row = id_row(a, 0, rows), id_row(b, 0, rows)
    a_col[...] = jnp.transpose(jnp.broadcast_to(a_row, (LANES, rows)))
    b_col[...] = jnp.transpose(jnp.broadcast_to(b_row, (LANES, rows)))
    for band in bands(rows, BAND):
        a_grad[band], a_loss[band] = add_band(a, b[:rows], a_col, b_row, sb, band)
    for band in bands(rows, BAND):
        b_grad[band], b_loss[band] = add_band(b, a[:rows], b_col, a_row, sb, band)


def gate_kernel(theirs, after, out):
    pass


def add_kernel(theirs, mine, col, sb, grad_in, loss_in, grad, loss):
    rows = grad.shape[0]
    their_ids = id_row(theirs, 0, rows)
    for band in bands(rows, BAND):
        more, losses = add_band(mine, theirs[:rows], col, their_ids, sb, band)
        grad[band] = grad_in[band] + more
        loss[band] = loss_in[band] + losses


def last_kernel(
    a_theirs, b_theirs, a, b, a_col, b_col, sb, a_grad, b_grad, a_loss, b_loss, a_raw, b_raw,
    image_grad, text_grad, row_loss, a_out, b_out, loss_scr, sems
):
    rows = a_grad.shape[0]
    even = even_blk()
    sides = (
        (0, a_theirs, a, a_col, a_grad, a_loss, a_raw, a_out, jnp.logical_not(even)),
        (1, b_theirs, b, b_col, b_grad, b_loss, b_raw, b_out, even),
    )
    for n, theirs, mine, col, grad, loss, raw, out, is_image in sides:
        their_ids = id_row(theirs, 0, rows)
        for band in bands(rows, BAND):
            more, losses = add_band(mine, theirs[:rows], col, their_ids, sb, band)
            losses = loss[band] + losses
            if n == 0:
                loss_scr[band] = losses
            else:
                loss_scr[band] = jnp.where(is_image, losses, loss_scr[band])
            out[band] = projected(raw[band], grad[band] + more)
            piece = band.start // BAND

            @pl.when(is_image)
            def _():
                pltpu.make_async_copy(out.at[band], image_grad.at[band], sems.at[n, piece]).start()

            @pl.when(jnp.logical_not(is_image))
            def _():
                pltpu.make_async_copy(out.at[band], text_grad.at[band], sems.at[n, piece]).start()

    row_loss[...] = (jnp.sum(jnp.transpose(loss_scr[...]), axis=0, keepdims=True) / (4 * rows)).reshape(rows)
    for n, _, _, _, _, _, _, out, _ in sides:
        for piece, band in enumerate(bands(rows, BAND)):
            pltpu.make_async_copy(out.at[band], image_grad.at[band], sems.at[n, piece]).wait()


def cost(rows, total, width, matmuls):
    return pl.CostEstimate(
        flops=matmuls * rows * total * width // 4, bytes_accessed=2 * total * width, transcendentals=2 * rows * total
    )


def in_vmem(array):
    return pltpu.with_memory_space_constraint(array, pltpu.VMEM)


def shards(images, texts, image_ids, text_ids, logit_scale, logit_bias):
    rows, width = images.shape
    packed_rows = rows + ID_ROWS
    params = pltpu.CompilerParams(vmem_limit_bytes=12 * 1024 * 1024)
    last_params = pltpu.CompilerParams(vmem_limit_bytes=18 * 1024 * 1024)
    sb = jnp.concatenate([logit_scale, logit_bias])
    grad = pltpu.VMEM((rows, width), F32)
    lanes = pltpu.VMEM((rows, LANES), F32)
    packed = pltpu.VMEM((packed_rows, width), BF16)
    raw = pltpu.VMEM((rows, width), BF16)
    a_blk, b_blk, a_group, b_group = routes(lax.axis_size("blk"), lax.axis_size("group"))

    def prep(is_a):
        return pl.pallas_call(
            functools.partial(prep_kernel, is_a),
            out_shape=(packed, raw),
            in_specs=[ANYWHERE, ANYWHERE, WHOLE, WHOLE],
            out_specs=[WHOLE] * 2,
            scratch_shapes=[pltpu.SemaphoreType.DMA((rows // PART,))],
            compiler_params=params,
            name="prep",
        )(texts, images, text_ids, image_ids)

    def gate(theirs, after):
        return pl.pallas_call(
            gate_kernel,
            out_shape=packed,
            in_specs=[ANYWHERE] * 2,
            out_specs=ANYWHERE,
            input_output_aliases={0: 0},
            compiler_params=params,
            name="gate",
        )(in_vmem(theirs), after)

    def add(theirs, mine, col, grad_in, loss_in, name):
        return pl.pallas_call(
            add_kernel,
            out_shape=(grad, lanes),
            in_specs=[WHOLE] * 3 + [SCALAR] + [WHOLE] * 2,
            out_specs=[WHOLE] * 2,
            input_output_aliases={4: 0, 5: 1},
            compiler_params=params,
            cost_estimate=cost(rows, rows, width, 2),
            name=name,
        )(in_vmem(theirs), in_vmem(mine), in_vmem(col), sb, in_vmem(grad_in), in_vmem(loss_in))

    a, a_raw = prep(True)
    a_near = lax.ppermute(a, BOTH, a_blk)
    b, b_raw = prep(False)
    b_near = lax.ppermute(b, BOTH, b_blk)
    a_hop = lax.ppermute(a, BOTH, a_group)
    b_hop = lax.ppermute(b, BOTH, b_group)
    a_grad, b_grad, a_loss, b_loss, a_col, b_col = pl.pallas_call(
        own_kernel,
        out_shape=(grad, grad, lanes, lanes, lanes, lanes),
        in_specs=[WHOLE] * 2 + [SCALAR],
        out_specs=[WHOLE] * 6,
        compiler_params=params,
        cost_estimate=cost(rows, rows, width, 4),
        name="own",
    )(in_vmem(a), in_vmem(b), sb)
    a_near = gate(a_near, a_loss)
    b_far = lax.ppermute(a_near, BOTH, b_blk)
    b_near = gate(b_near, a_near)
    a_far = lax.ppermute(b_near, BOTH, a_blk)
    a_grad, a_loss = add(a_near, a, a_col, a_grad, a_loss, "neara")
    b_grad, b_loss = add(b_near, b, b_col, b_grad, b_loss, "nearb")
    b_grad, b_loss = add(b_far, b, b_col, b_grad, b_loss, "farb")
    a_grad, a_loss = add(a_far, a, a_col, a_grad, a_loss, "fara")
    image_grad, text_grad, row_loss = pl.pallas_call(
        last_kernel,
        out_shape=(
            jax.ShapeDtypeStruct((rows, width), F32),
            jax.ShapeDtypeStruct((rows, width), F32),
            jax.ShapeDtypeStruct((rows,), F32),
        ),
        in_specs=[WHOLE] * 6 + [SCALAR] + [WHOLE] * 6,
        out_specs=[ANYWHERE, ANYWHERE, WHOLE],
        scratch_shapes=[
            pltpu.VMEM((rows, width), F32),
            pltpu.VMEM((rows, width), F32),
            pltpu.VMEM((rows, LANES), F32),
            pltpu.SemaphoreType.DMA((2, rows // BAND)),
        ],
        compiler_params=last_params,
        cost_estimate=cost(rows, rows, width, 4),
        name="last",
    )(
        in_vmem(b_hop), in_vmem(a_hop), in_vmem(a), in_vmem(b), in_vmem(a_col), in_vmem(b_col), sb, in_vmem(a_grad),
        in_vmem(b_grad), in_vmem(a_loss), in_vmem(b_loss), in_vmem(a_raw), in_vmem(b_raw)
    )
    return (row_loss, image_grad, text_grad)


def solution(mesh):
    placed = (
        P(("blk", "group"), None),
        P(("blk", "group"), None),
        P(("blk", "group")),
        P(("blk", "group")),
        P(),
        P(),
    )
    return jax.shard_map(
        shards,
        mesh=mesh,
        in_specs=placed,
        out_specs=(P(("blk", "group")), P(("blk", "group"), None), P(("blk", "group"), None)),
        check_vma=False,
    )
```

```python
import functools

import jax
import jax.numpy as jnp
from jax import lax
from jax.experimental import pallas as pl
from jax.experimental.pallas import tpu as pltpu
from jax.sharding import PartitionSpec as P

WHOLE = pl.BlockSpec(memory_space=pltpu.VMEM)
SCALAR = pl.BlockSpec(memory_space=pltpu.SMEM)
ANYWHERE = pl.BlockSpec(memory_space=pl.ANY)
LANES = 128
ID_ROWS = 16
BAND = 320
PART = 160
CUT = 320
F32, BF16 = jnp.float32, jnp.bfloat16
BOTH = ("blk", "group")


BY_WAY = {0: 1, 7: 6}


def routes(blks, groups):
    out = [[], [], [], [], []]
    for p in range(blks):
        for q in range(groups):
            here, up, plane = p * groups + q, 1 if p % 2 == 0 else -1, p % 8
            out[0].append((here, (p + up) % blks * groups + q))
            out[1].append((here, (p - up) % blks * groups + q))
            target = p * groups + (q + 1) % groups
            if q % 2 and plane in BY_WAY:
                middle = target + (BY_WAY[plane] - plane) * groups
                out[2].append((here, middle))
                out[3].append((middle, target))
            elif q % 2 and plane in BY_WAY.values():
                out[3].append((here, target))
            else:
                out[2].append((here, target))
            out[4].append((here, p * groups + (q - 1) % groups))
    return out


def even_blk():
    return lax.rem(lax.axis_index("blk"), 2) == 0


def even_group():
    return lax.rem(lax.axis_index("group"), 2) == 0


def in_planes(planes):
    plane = lax.rem(lax.axis_index("blk"), 8)
    first, second = planes
    return jnp.logical_or(plane == first, plane == second)


def unit_rows(values):
    full = values.astype(F32)
    return full * lax.rsqrt(jnp.sum(full * full, axis=-1, keepdims=True) + 1e-06)


def projected(values, grad):
    full = values.astype(F32)
    scales = lax.rsqrt(jnp.sum(full * full, axis=-1, keepdims=True) + 1e-06)
    along = jnp.sum(full * grad, axis=1, keepdims=True)
    return grad * scales - full * (along * (scales * scales * scales))


def score_block(mine, theirs, my_ids, their_ids, scale, bias):
    dots = lax.dot_general(mine, theirs, (((1,), (1,)), ((), ())), preferred_element_type=F32)
    turn = jnp.where(my_ids == their_ids, -1.0, 1.0)
    power = jnp.exp(turn * (scale * dots + bias))
    whole = 1.0 + power
    coef = ((turn * scale) * (power * pl.reciprocal(whole, approx=True))).astype(BF16)
    return coef, power, whole


def softplus_sums(power, whole):
    values = jnp.where(power < 1e-3, power - 0.5 * power * power, jnp.log(whole))
    total = values[:, :LANES]
    for at in range(LANES, values.shape[1], LANES):
        total = total + values[:, at : at + LANES]
    return total


def bands(rows, size):
    return [slice(at, at + size) for at in range(0, rows, size)]


def id_row(packed, first, rows):
    at = packed.shape[0] - ID_ROWS
    return packed[at:, first : first + rows].astype(F32)[:1]


def prep_kernel(is_a, texts, images, text_ids, image_ids, packed, raw, sems):
    rows = raw.shape[0]
    texts_here = even_blk() if is_a else jnp.logical_not(even_blk())
    pieces = bands(rows, PART)

    @pl.when(texts_here)
    def _():
        for n, piece in enumerate(pieces):
            pltpu.make_async_copy(texts.at[piece], raw.at[piece], sems.at[n]).start()

    @pl.when(jnp.logical_not(texts_here))
    def _():
        for n, piece in enumerate(pieces):
            pltpu.make_async_copy(images.at[piece], raw.at[piece], sems.at[n]).start()

    ids = jnp.where(texts_here, text_ids[...].reshape(1, rows), image_ids[...].reshape(1, rows))
    packed[rows:] = jnp.zeros((ID_ROWS, packed.shape[1]), BF16)
    packed[rows:, :rows] = jnp.broadcast_to(ids.astype(F32), (ID_ROWS, rows)).astype(BF16)
    for n, piece in enumerate(pieces):
        pltpu.make_async_copy(texts.at[piece], raw.at[piece], sems.at[n]).wait()
        packed[piece] = unit_rows(raw[piece]).astype(BF16)


def add_band(mine, theirs, col, their_ids, sb, band):
    coef, power, whole = score_block(mine[band], theirs, col[band, :1], their_ids, sb[0], sb[1])
    return jnp.dot(coef, theirs, preferred_element_type=F32), softplus_sums(power, whole)


def split_kernel(a, b, text):
    @pl.when(even_blk())
    def _():
        text[...] = a[...]

    @pl.when(jnp.logical_not(even_blk()))
    def _():
        text[...] = b[...]


def own_kernel(a, b, sb, a_grad, b_grad, a_loss, b_loss, a_col, b_col):
    rows = a_grad.shape[0]
    a_row, b_row = id_row(a, 0, rows), id_row(b, 0, rows)
    a_col[...] = jnp.transpose(jnp.broadcast_to(a_row, (LANES, rows)))
    b_col[...] = jnp.transpose(jnp.broadcast_to(b_row, (LANES, rows)))
    for band in bands(rows, BAND):
        a_grad[band], a_loss[band] = add_band(a, b[:rows], a_col, b_row, sb, band)
    for band in bands(rows, BAND):
        b_grad[band], b_loss[band] = add_band(b, a[:rows], b_col, a_row, sb, band)


def gate_kernel(theirs, after, out):
    pass


def add_kernel(theirs, mine, col, sb, grad_in, loss_in, after, grad, loss):
    rows = grad.shape[0]
    their_ids = id_row(theirs, 0, rows)
    for band in bands(rows, BAND):
        more, losses = add_band(mine, theirs[:rows], col, their_ids, sb, band)
        grad[band] = grad_in[band] + more
        loss[band] = loss_in[band] + losses


def turn_kernel(own_text, come, a, b, after, upper, lower, image):
    @pl.when(even_blk())
    def _():
        image[...] = b[...]

    @pl.when(jnp.logical_not(even_blk()))
    def _():
        image[...] = a[...]

    own = jnp.logical_and(in_planes(tuple(BY_WAY.values())), jnp.logical_not(even_group()))
    half = upper.shape[0]

    @pl.when(own)
    def _():
        upper[...] = own_text[:half]
        lower[...] = own_text[half:]

    @pl.when(jnp.logical_not(own))
    def _():
        upper[...] = come[:half]
        lower[...] = come[half:]


def text_hop_kernel(
    direct, upper, lower, a, b, a_col, b_col, sb, a_grad_in, b_grad_in, a_loss_in, b_loss_in,
    a_grad, b_grad, a_loss, b_loss, chosen
):
    half, rows = upper.shape[0], a_grad.shape[0]
    by_way = jnp.logical_and(in_planes(tuple(BY_WAY)), even_group())
    by_way = jnp.logical_or(by_way, jnp.logical_and(in_planes(tuple(BY_WAY.values())), even_group()))

    @pl.when(by_way)
    def _():
        chosen[:half] = upper[...]
        chosen[half:] = lower[...]

    @pl.when(jnp.logical_not(by_way))
    def _():
        chosen[...] = direct[...]

    @pl.when(even_blk())
    def _():
        add_kernel(chosen, b, b_col, sb, b_grad_in, b_loss_in, None, b_grad, b_loss)

    @pl.when(jnp.logical_not(even_blk()))
    def _():
        add_kernel(chosen, a, a_col, sb, a_grad_in, a_loss_in, None, a_grad, a_loss)


def last_kernel(
    theirs, a, b, a_col, b_col, sb, a_grad, b_grad, a_loss, b_loss, a_raw, b_raw,
    image_grad, text_grad, row_loss, image_out, text_out, sems
):
    rows = a_grad.shape[0]
    pieces = bands(rows, BAND)

    def finish(image_sum, image_raw, image_loss, text, text_col, text_sum, text_raw):
        for n, band in enumerate(pieces):
            image_out[band] = projected(image_raw[band], image_sum[band])
            pltpu.make_async_copy(image_out.at[band], image_grad.at[band], sems.at[0, n]).start()
        their_ids = id_row(theirs, 0, rows)
        for n, band in enumerate(pieces):
            coef, _, _ = score_block(text[band], theirs[:rows], text_col[band, :1], their_ids, sb[0], sb[1])
            total = text_sum[band] + jnp.dot(coef, theirs[:rows], preferred_element_type=F32)
            text_out[band] = projected(text_raw[band], total)
            pltpu.make_async_copy(text_out.at[band], text_grad.at[band], sems.at[1, n]).start()
        sums = jnp.sum(jnp.transpose(image_loss[...]), axis=0, keepdims=True)
        row_loss[...] = (sums / (4 * rows)).reshape(rows)

    @pl.when(even_blk())
    def _():
        finish(b_grad, b_raw, b_loss, a, a_col, a_grad, a_raw)

    @pl.when(jnp.logical_not(even_blk()))
    def _():
        finish(a_grad, a_raw, a_loss, b, b_col, b_grad, b_raw)

    for n, band in enumerate(pieces):
        pltpu.make_async_copy(image_out.at[band], image_grad.at[band], sems.at[0, n]).wait()
        pltpu.make_async_copy(text_out.at[band], text_grad.at[band], sems.at[1, n]).wait()


def cost(rows, total, width, matmuls):
    return pl.CostEstimate(
        flops=matmuls * rows * total * width // 4, bytes_accessed=2 * total * width, transcendentals=2 * rows * total
    )


def in_vmem(array):
    return pltpu.with_memory_space_constraint(array, pltpu.VMEM)


def shards(images, texts, image_ids, text_ids, logit_scale, logit_bias):
    rows, width = images.shape
    packed_rows = rows + ID_ROWS
    params = pltpu.CompilerParams(vmem_limit_bytes=12 * 1024 * 1024)
    last_params = pltpu.CompilerParams(vmem_limit_bytes=18 * 1024 * 1024)
    sb = jnp.concatenate([logit_scale, logit_bias])
    grad = pltpu.VMEM((rows, width), F32)
    lanes = pltpu.VMEM((rows, LANES), F32)
    packed = pltpu.VMEM((packed_rows, width), BF16)
    raw = pltpu.VMEM((rows, width), BF16)
    a_blk, b_blk, text_first, text_second, image_route = routes(lax.axis_size("blk"), lax.axis_size("group"))

    def prep(is_a):
        return pl.pallas_call(
            functools.partial(prep_kernel, is_a),
            out_shape=(packed, raw),
            in_specs=[ANYWHERE, ANYWHERE, WHOLE, WHOLE],
            out_specs=[WHOLE] * 2,
            scratch_shapes=[pltpu.SemaphoreType.DMA((rows // PART,))],
            compiler_params=params,
            name="prep",
        )(texts, images, text_ids, image_ids)

    def gate(theirs, after):
        return pl.pallas_call(
            gate_kernel,
            out_shape=packed,
            in_specs=[ANYWHERE] * 2,
            out_specs=ANYWHERE,
            input_output_aliases={0: 0},
            compiler_params=params,
            name="gate",
        )(in_vmem(theirs), after)

    def add(theirs, mine, col, grad_in, loss_in, after, name):
        return pl.pallas_call(
            add_kernel,
            out_shape=(grad, lanes),
            in_specs=[WHOLE] * 3 + [SCALAR] + [WHOLE] * 2 + [ANYWHERE],
            out_specs=[WHOLE] * 2,
            input_output_aliases={4: 0, 5: 1},
            compiler_params=params,
            cost_estimate=cost(rows, rows, width, 2),
            name=name,
        )(in_vmem(theirs), in_vmem(mine), in_vmem(col), sb, in_vmem(grad_in), in_vmem(loss_in), after)

    a, a_raw = prep(True)
    a_near = lax.ppermute(a, BOTH, a_blk)
    b, b_raw = prep(False)
    b_near = lax.ppermute(b, BOTH, b_blk)
    text = pl.pallas_call(
        split_kernel,
        out_shape=packed,
        in_specs=[WHOLE] * 2,
        out_specs=WHOLE,
        compiler_params=params,
        name="split",
    )(in_vmem(a), in_vmem(b))
    text_hop = lax.ppermute(text, BOTH, text_first)
    a_grad, b_grad, a_loss, b_loss, a_col, b_col = pl.pallas_call(
        own_kernel,
        out_shape=(grad, grad, lanes, lanes, lanes, lanes),
        in_specs=[WHOLE] * 2 + [SCALAR],
        out_specs=[WHOLE] * 6,
        compiler_params=params,
        cost_estimate=cost(rows, rows, width, 4),
        name="own",
    )(in_vmem(a), in_vmem(b), sb)
    a_near = gate(a_near, a_loss)
    b_far = lax.ppermute(a_near, BOTH, b_blk)
    b_near = gate(b_near, a_near)
    a_far = lax.ppermute(b_near, BOTH, a_blk)
    *turned, image = pl.pallas_call(
        turn_kernel,
        out_shape=(pltpu.VMEM((CUT, width), BF16), pltpu.VMEM((packed_rows - CUT, width), BF16), packed),
        in_specs=[WHOLE] * 4 + [ANYWHERE],
        out_specs=[WHOLE] * 3,
        compiler_params=params,
        name="turn",
    )(in_vmem(text), in_vmem(text_hop), in_vmem(a), in_vmem(b), a_near)
    text_parts = [lax.ppermute(part, BOTH, text_second) for part in turned]
    image_hop = lax.ppermute(image, BOTH, image_route)
    a_grad, a_loss = add(a_near, a, a_col, a_grad, a_loss, a_loss, "neara")
    b_grad, b_loss = add(b_near, b, b_col, b_grad, b_loss, a_loss, "nearb")
    b_grad, b_loss = add(b_far, b, b_col, b_grad, b_loss, a_loss, "farb")
    a_grad, a_loss = add(a_far, a, a_col, a_grad, a_loss, b_loss, "fara")
    a_grad, b_grad, a_loss, b_loss = pl.pallas_call(
        text_hop_kernel,
        out_shape=(grad, grad, lanes, lanes),
        in_specs=[WHOLE] * 7 + [SCALAR] + [WHOLE] * 4,
        out_specs=[WHOLE] * 4,
        scratch_shapes=[pltpu.VMEM((packed_rows, width), BF16)],
        input_output_aliases={8: 0, 9: 1, 10: 2, 11: 3},
        compiler_params=params,
        cost_estimate=cost(rows, rows, width, 2),
        name="hopt",
    )(
        in_vmem(text_hop), in_vmem(text_parts[0]), in_vmem(text_parts[1]), in_vmem(a), in_vmem(b), in_vmem(a_col),
        in_vmem(b_col), sb, in_vmem(a_grad), in_vmem(b_grad), in_vmem(a_loss), in_vmem(b_loss)
    )
    image_grad, text_grad, row_loss = pl.pallas_call(
        last_kernel,
        out_shape=(
            jax.ShapeDtypeStruct((rows, width), F32),
            jax.ShapeDtypeStruct((rows, width), F32),
            jax.ShapeDtypeStruct((rows,), F32),
        ),
        in_specs=[WHOLE] * 5 + [SCALAR] + [WHOLE] * 6,
        out_specs=[ANYWHERE, ANYWHERE, WHOLE],
        scratch_shapes=[
            pltpu.VMEM((rows, width), F32),
            pltpu.VMEM((rows, width), F32),
            pltpu.SemaphoreType.DMA((2, rows // BAND)),
        ],
        compiler_params=last_params,
        cost_estimate=cost(rows, rows, width, 2),
        name="last",
    )(
        in_vmem(image_hop), in_vmem(a), in_vmem(b), in_vmem(a_col), in_vmem(b_col), sb, in_vmem(a_grad),
        in_vmem(b_grad), in_vmem(a_loss), in_vmem(b_loss), in_vmem(a_raw), in_vmem(b_raw)
    )
    return (row_loss, image_grad, text_grad)


def solution(mesh):
    placed = (
        P(("blk", "group"), None),
        P(("blk", "group"), None),
        P(("blk", "group")),
        P(("blk", "group")),
        P(),
        P(),
    )
    return jax.shard_map(
        shards,
        mesh=mesh,
        in_specs=placed,
        out_specs=(P(("blk", "group")), P(("blk", "group"), None), P(("blk", "group"), None)),
        check_vma=False,
    )
```
